1024 devices in a mesh: ax: 256 (over z, x, y_lo), rad: 4 (over y_hi, core).
Axes of the slice: x: 4, y: 8 (y_hi: 2, y_lo: 4; y = y_hi * 4 + y_lo), z: 16, core: 2. Of those that a mesh axis runs over, the one named last changes fastest.
Arguments:
- forcing_state: bfloat16 [512, 64, 16, 320], P('ax', 'rad'), may hold values from -6 to 6
- link_bits: int32 [512, 64, 4], P('ax', 'rad'), may hold values from 0 to 1, as said below
- couplings: bfloat16 [5, 320, 320], replicated, may hold values from -0.15625 to 0.15625
- shape_vectors: bfloat16 [512, 64, 320], P('ax', 'rad'), may hold values from -0.3125 to 0.3125
- actuator_map: int32 [512, 64], P('ax', 'rad'), may hold values from 0 to 4095, as said below
Outputs:
- adjoint_state: bfloat16 [512, 64, 16, 320], P('ax', 'rad')
- actuator_grad: float32 [16, 4096], P(None, ('ax', 'rad'))
The draws below stay inside these ranges and needn't reach their ends.
Inputs may be any that keep to these rules, and one draw needn't show every extreme that they name: The pattern is symmetric: link_bits[i, j, 1] equals link_bits[i + 1, j, 0] and link_bits[i, j, 3] equals link_bits[i, j + 1, 2]. `actuator_map`: actuator a lies in the group a // 4; the group of block (i, j)'s actuator is (i // 2 + d) * 4 + j // 16 with d one of -1, 0, 1.
All inputs are finite; a program needn't handle non-finite values.
Results may differ from the reference program's by a relative error of at most 0.0065.
Values may be sent and summed in bfloat16 or wider, within the bound.
No kernel may reach another device: no remote copies, remote signals or barrier semaphores. Data moves between devices by JAX's collectives and lax.ppermute only.
A program may use at most 32 MiB of HBM per device.

```python
import jax
import jax.numpy as jnp

DOF = 320
FORC = 16
ACT = 4096
STEPS = 2
AXB = 2
RADB = 16
NX = 512
NY = 64


def draw_link_bits(key, part):
    key = jax.random.fold_in(key, 11)
    key_axial, key_radial = jax.random.split(key)
    axial = (jax.random.randint(key_axial, (NX + 1, NY), 0, 4) < 3).astype(jnp.int32)
    radial = (jax.random.randint(key_radial, (NX, NY + 1), 0, 4) < 3).astype(jnp.int32)
    return jnp.stack([axial[:-1], axial[1:], radial[:, :-1], radial[:, 1:]], axis=-1)


def draw_actuator_map(key, part):
    key = jax.random.fold_in(key, 23)
    key_shift, key_slot = jax.random.split(key)
    groups_ax = NX // AXB
    groups_rad = NY // RADB
    per_group = ACT // (groups_ax * groups_rad)
    slab = (jnp.arange(NX, dtype=jnp.int32) // AXB)[:, None]
    cycle = (jnp.arange(NY, dtype=jnp.int32) // RADB)[None, :]
    offset = jax.random.randint(key_shift, (NX, NY), -1, 2)
    target = jnp.clip(slab + offset, 0, groups_ax - 1)
    slot = jax.random.randint(key_slot, (NX, NY), 0, per_group)
    return ((target * groups_rad + cycle) * per_group + slot).astype(jnp.int32)


def block_scale(stream_key, extent, cuts, smallest, high):
    gain, own = 1.0, jax.random.fold_in(stream_key, 6)
    for position, blocks in cuts:
        steps = jnp.exp(jax.random.uniform(jax.random.fold_in(own, position), (blocks,), jnp.float32, smallest / len(cuts), high / len(cuts)))
        gain = gain * jnp.repeat(steps, extent[position] // blocks).reshape([-1 if axis == position else 1 for axis in range(len(extent))])
    return gain


def scatter_about(rng, dims, scale, bound, cuts=(), kind=jnp.bfloat16):
    entries = jax.random.normal(rng, dims, jnp.float32) * scale
    if len(cuts) > 0:
        entries = block_scale(rng, dims, cuts, -0.22, 0.18) * entries
    return jnp.clip(entries, min=-bound, max=bound).astype(kind)


def setup_inputs(seed: int = 0) -> dict:
    key_list = jax.random.split(jax.random.key(seed), 6)
    forcing_state = scatter_about(key_list[0], (NX, NY, FORC, DOF), 1.0, 6.0, ((0, 256), (1, 4)))
    link_bits = draw_link_bits(jax.random.fold_in(key_list[5], 71), 0)
    couplings = scatter_about(key_list[2], (5, DOF, DOF), (4 * DOF) ** -0.5, 0.15625)
    shape_vectors = scatter_about(key_list[3], (NX, NY, DOF), DOF ** -0.5, 0.3125, ((0, 256), (1, 4)))
    actuator_map = draw_actuator_map(jax.random.fold_in(key_list[5], 71), 0)
    return dict(forcing_state=forcing_state, link_bits=link_bits, couplings=couplings, shape_vectors=shape_vectors, actuator_map=actuator_map)


def neighbour_fields(field_now):
    padded = jnp.pad(field_now, ((1, 1), (1, 1), (0, 0), (0, 0)))
    return [padded[:-2, 1:-1], padded[2:, 1:-1], padded[1:-1, :-2], padded[1:-1, 2:]]


def couple(field_now, matrix):
    flat = field_now.reshape(-1, field_now.shape[-1])
    summed = jnp.dot(flat, matrix, preferred_element_type=jnp.float32)
    return summed.reshape(field_now.shape[:-1] + (matrix.shape[1],))


def advance(field_now, link_bits, couplings, adjoint):
    opposite = [1, 0, 3, 2]
    masks = link_bits.astype(jnp.float32)
    if adjoint:
        summed = couple(field_now, couplings[0].T)
    else:
        summed = couple(field_now, couplings[0])
    beside = neighbour_fields(field_now)
    for direction in range(4):
        if adjoint:
            matrix = couplings[opposite[direction] + 1].T
        else:
            matrix = couplings[direction + 1]
        summed = summed + masks[:, :, direction][:, :, None, None] * couple(beside[direction], matrix)
    return summed.astype(jnp.bfloat16)


def reference(forcing_state, link_bits, couplings, shape_vectors, actuator_map):
    field_now = forcing_state
    for repeat in range(STEPS):
        field_now = advance(field_now, link_bits, couplings, False)
    for repeat in range(STEPS):
        field_now = advance(field_now, link_bits, couplings, True)
    projected = jnp.einsum("xyfk,xyk->xyf", field_now.astype(jnp.float32), shape_vectors.astype(jnp.float32))
    grad_rows = jax.ops.segment_sum(projected.reshape(-1, projected.shape[-1]), actuator_map.reshape(-1), num_segments=ACT)
    return field_now, grad_rows.T
```

```python
import jax
import jax.numpy as jnp
from jax import lax
from jax.sharding import Mesh, PartitionSpec as P

ACT = 4096
STEPS = 2
DOF = 320
FORC = 16
RING = 4
WIDE = 384
HALO = 6
BF = jnp.bfloat16


def body(state, bits, couplings, shapes, amap):
    n_h, n_rad = lax.axis_size("h"), lax.axis_size("r")
    h, y, r = lax.axis_index("h"), lax.axis_index("y"), lax.axis_index("r")
    axb, radb = state.shape[:2]
    blocks = axb * radb
    per_group = ACT // (n_h * RING * n_rad)
    ahead = [(i, i + 1) for i in range(n_h - 1)]
    back = [(b, a) for a, b in ahead]

    edge = []
    for i in range(n_h - 1):
        edge.append((i * RING + RING - 1, (i + 1) * RING + RING - 1))
        edge.append(((i + 1) * RING, i * RING))
    beside = lax.ppermute(shapes, ("h", "y"), edge)
    vecs = lax.all_gather(jnp.stack([shapes, beside]), ("y", "r"))
    vecs = vecs.reshape(RING, n_rad, 2, axb, radb, DOF).transpose(0, 2, 3, 1, 4, 5)
    vecs = jnp.concatenate([vecs[-1:, 1], vecs[:, 0], vecs[:1, 1]], 0)
    vecs = vecs.reshape((RING + 2) * axb, n_rad * radb, DOF)

    group_of = amap // per_group
    shift = (group_of - ((h * RING + y) * n_rad + r)) // n_rad
    column = (shift + 1) * per_group + amap % per_group
    meta = jnp.concatenate([bits, column[..., None]], -1).astype(BF).reshape(1, blocks, 5)
    send = state.transpose(2, 0, 1, 3).reshape(FORC, blocks, DOF)
    send = jnp.concatenate([send, jnp.broadcast_to(meta, (FORC, blocks, 5)), jnp.zeros((FORC, blocks, WIDE - DOF - 5), BF)], -1)
    mine = lax.all_to_all(send, ("y", "r"), 0, 0, tiled=True)
    low = lax.ppermute(mine[n_rad:], "h", ahead)
    high = lax.ppermute(mine[:-n_rad], "h", back)
    window = jnp.concatenate([low, mine, high], 0)
    slabs = window.shape[0] // n_rad
    window = window.reshape(slabs, n_rad, axb, radb, WIDE).transpose(0, 2, 1, 3, 4).reshape(slabs * axb, n_rad * radb, WIDE)
    field = window[..., :DOF]
    masks = window[..., DOF : DOF + 4].astype(jnp.float32)
    column = window[..., DOF + 4].astype(jnp.int32)

    opposite = [1, 0, 3, 2]
    for step in range(2 * STEPS):
        adjoint = step >= STEPS
        dims = (((2,), (1 if adjoint else 0,)), ((), ()))
        mid = field[1:-1]
        side = jnp.pad(mid, ((0, 0), (1, 1), (0, 0)))
        near = [field[:-2], field[2:], side[:, :-2], side[:, 2:]]
        masks = masks[1:-1]
        total = lax.dot_general(mid, couplings[0], dims, preferred_element_type=jnp.float32)
        for e in range(4):
            matrix = couplings[opposite[e] + 1] if adjoint else couplings[e + 1]
            total = total + masks[:, :, e : e + 1] * lax.dot_general(near[e], matrix, dims, preferred_element_type=jnp.float32)
        field = total.astype(BF)

    cut = 2 * STEPS
    rows = field.shape[0]
    column = column[cut : cut + rows]
    proj = jnp.einsum("xyk,xyk->xy", field, vecs, preferred_element_type=jnp.float32)
    slab = jnp.arange(rows, dtype=jnp.int32)[:, None] // axb - 1
    cycle = jnp.arange(n_rad * radb, dtype=jnp.int32)[None, :] // radb
    target = ((slab + column // per_group - 1) * n_rad + cycle) * per_group + column % per_group
    hot = (target.reshape(-1, 1) == jnp.arange(RING * n_rad * per_group, dtype=jnp.int32)[None]).astype(jnp.float32)
    grad = jnp.sum(proj.reshape(-1, 1) * hot, 0).reshape(FORC, per_group)
    top = lax.reduce_precision(grad, 8, 7)
    tail = jnp.concatenate([top, grad - top], -1).astype(BF)
    tail = jnp.pad(tail[:, None], ((0, 0), (0, blocks - 1), (0, WIDE - DOF - 2 * per_group)))
    own = field[axb:-axb].reshape(RING, axb, n_rad, radb, DOF).transpose(0, 2, 1, 3, 4).reshape(FORC, blocks, DOF)
    back_home = lax.all_to_all(jnp.concatenate([own, tail], -1), ("y", "r"), 0, 0, tiled=True)
    result = back_home[..., :DOF].reshape(FORC, axb, radb, DOF).transpose(1, 2, 0, 3)
    tail = back_home[:, 0, DOF : DOF + 2 * per_group].astype(jnp.float32)
    return result, tail[:, :per_group] + tail[:, per_group:]


def solution(mesh):
    n_ax, n_rad = mesh.shape["ax"], mesh.shape["rad"]
    fine = Mesh(mesh.devices.reshape(n_ax // RING, RING, n_rad), ("h", "y", "r"))
    ax = ("h", "y")
    in_specs = (P(ax, "r"), P(ax, "r"), P(), P(ax, "r"), P(ax, "r"))
    out_specs = (P(ax, "r"), P(None, ("h", "y", "r")))
    return jax.shard_map(body, mesh=fine, in_specs=in_specs, out_specs=out_specs, check_vma=False)
```

```python
import functools

import jax
import jax.numpy as jnp
from jax import lax
from jax.experimental import pallas as pl
from jax.experimental.pallas import tpu as pltpu
from jax.sharding import Mesh, PartitionSpec as P

ACT = 4096
STEPS = 2
DOF = 320
FORC = 16
RING = 4
AXB = 2
RADB = 16
BLOCKS = AXB * RADB
WIDE = 384
MAIN = 256
HALO = 2 * STEPS
BF = jnp.bfloat16
F32 = jnp.float32
ROWS = FORC * BLOCKS
NRAD = 4
LINE = NRAD * RADB
WINDOW = RING * AXB + 2 * HALO
DEPTH = 5 * MAIN + WIDE
PACKED = 80


def iota(shape, dim):
    return lax.broadcasted_iota(jnp.int32, shape, dim)


def one_hot(rows, cols, of_row):
    return jnp.where(iota((rows, cols), 1) == of_row(iota((rows, cols), 0)), 1.0, 0.0).astype(BF)


def dot(a, b):
    return jnp.dot(a, b, preferred_element_type=F32)


def pack_kernel(state_ref, bits_ref, out_ref, wide):
    wide[...] = jnp.zeros_like(wide)
    wide[:, :DOF] = state_ref[...]
    order = one_hot(ROWS, ROWS, lambda o: (o % BLOCKS) * FORC + o // BLOCKS)
    block = one_hot(ROWS, BLOCKS, lambda o: o % BLOCKS)
    out = dot(order, wide[...]) + dot(block, bits_ref[...])
    out_ref[...] = out.astype(BF).reshape(FORC, BLOCKS, WIDE)


def pack(state, bits):
    return pl.pallas_call(
        pack_kernel,
        out_shape=jax.ShapeDtypeStruct((FORC, BLOCKS, WIDE), BF),
        scratch_shapes=[pltpu.VMEM((ROWS, WIDE), BF)],
        compiler_params=pltpu.CompilerParams(vmem_limit_bytes=32 * 1024 * 1024),
        name="pack",
    )(state, bits)


def steps_kernel(low_ref, mine_ref, high_ref, fore_ref, adj_ref, out_ref, s_a, s_b, left, right, masks):
    total = WINDOW * LINE
    for i in range(WINDOW):
        for r in range(NRAD):
            if i < HALO:
                ref, at = low_ref, i
            elif i < WINDOW - HALO:
                ref, at = mine_ref, i - HALO
            else:
                ref, at = high_ref, i - (WINDOW - HALO)
            slot, half = (at // AXB) * NRAD + r, at % AXB
            row = i * LINE + r * RADB
            s_a[row : row + RADB, :] = ref[slot, half * RADB : (half + 1) * RADB, :]
    pick = jnp.where(iota((128, 512), 0) == 64 + iota((128, 512), 1) // 128, 1.0, 0.0).astype(BF)
    spread = dot(s_a[:, MAIN:], pick)
    place = iota((total, 128), 0) % LINE
    masks[:, :256] = spread[:, :256].astype(BF)
    masks[:, 256:384] = jnp.where(place > 0, spread[:, 256:384], 0.0).astype(BF)
    masks[:, 384:] = jnp.where(place < LINE - 1, spread[:, 384:], 0.0).astype(BF)
    tail = s_a[:, MAIN:].astype(F32)
    tail = jnp.where(iota((total, 128), 1) < 64, tail, pltpu.roll(tail, 64, 1))
    s_a[:, MAIN:] = tail.astype(BF)

    def sides(value, a, b):
        down, up = pltpu.roll(value, 1, 0).astype(BF), pltpu.roll(value, b - a - 1, 0).astype(BF)
        for t in range(3):
            cols = slice(128 * t, 128 * t + 128)
            left[a:b, cols] = down[:, cols] * masks[a:b, 256:384]
            right[a:b, cols] = up[:, cols] * masks[a:b, 384:]

    a, b = LINE, total - LINE
    for c in range(a, b, 7 * LINE):
        sides(s_a[c : c + 7 * LINE, :].astype(F32), c, c + 7 * LINE)

    now, later = s_a, s_b
    for step in range(2 * STEPS):
        weights = fore_ref if step < STEPS else adj_ref
        first, last = step + 1, WINDOW - step - 1
        chunk = (last - first) // 2
        for i in range(first, last, chunk):
            a, b = i * LINE, (i + chunk) * LINE
            first_half = iota((b - a, 128), 1) < 64
            m0, m1 = masks[a:b, :128], masks[a:b, 128:256]
            prev, own, nxt = now[a - LINE : b - LINE, :], now[a:b, :], now[a + LINE : b + LINE, :]
            lhs = jnp.concatenate(
                [
                    own[:, :MAIN],
                    prev[:, :128] * m0,
                    prev[:, 128:256] * m0,
                    nxt[:, :128] * m1,
                    nxt[:, 128:256] * m1,
                    left[a:b, :MAIN],
                    right[a:b, :MAIN],
                    jnp.where(first_half, own[:, MAIN:], prev[:, MAIN:] * m0),
                    jnp.where(first_half, nxt[:, MAIN:] * m1, left[a:b, MAIN:]),
                    right[a:b, MAIN:],
                ],
                axis=1,
            )
            value = dot(lhs, weights[...])
            later[a:b, :] = value.astype(BF)
            if step < 2 * STEPS - 1:
                sides(value, a, b)
        now, later = later, now

    early = iota((RADB, 128), 1) < 64
    for y in range(RING):
        for r in range(NRAD):
            rows = [(HALO + y * AXB + half) * LINE + r * RADB for half in range(AXB)]
            slot = y * NRAD + r
            for half, row in enumerate(rows):
                out_ref[slot, half * RADB : (half + 1) * RADB, :] = now[row : row + RADB, :128]
                out_ref[slot, BLOCKS + half * RADB : BLOCKS + (half + 1) * RADB, :] = now[row : row + RADB, 128:256]
            out_ref[slot, 2 * BLOCKS :, :] = jnp.where(early, now[rows[0] : rows[0] + RADB, MAIN:], now[rows[1] : rows[1] + RADB, MAIN:])


def steps(low, mine, high, fore, adj):
    field = pltpu.VMEM((WINDOW * LINE, WIDE), BF)
    return pl.pallas_call(
        steps_kernel,
        out_shape=jax.ShapeDtypeStruct((FORC, PACKED, 128), BF),
        scratch_shapes=[field, field, field, field, pltpu.VMEM((WINDOW * LINE, 512), BF)],
        compiler_params=pltpu.CompilerParams(vmem_limit_bytes=48 * 1024 * 1024),
        name="steps",
    )(low, mine, high, fore, adj)


def unpack_kernel(back_ref, shapes_ref, hot_ref, state_ref, prev_ref, own_ref, next_ref, wide):
    for f in range(FORC):
        row = f * BLOCKS
        wide[row : row + BLOCKS, :128] = back_ref[f, :BLOCKS, :]
        wide[row : row + BLOCKS, 128:256] = back_ref[f, BLOCKS : 2 * BLOCKS, :]
        tail = back_ref[f, 2 * BLOCKS :, :]
        wide[row : row + RADB, MAIN:] = tail
        wide[row + RADB : row + BLOCKS, MAIN:] = pltpu.roll(tail.astype(F32), 64, 1).astype(BF)
    order = one_hot(ROWS, ROWS, lambda o: (o % FORC) * BLOCKS + o // FORC)
    state = dot(order, wide[...])[:, :DOF]
    state_ref[...] = state.astype(BF)
    block = one_hot(ROWS, BLOCKS, lambda o: o // FORC)
    proj = jnp.sum(state * dot(block, shapes_ref[...]), axis=1, keepdims=True)
    part = proj * dot(block, hot_ref[...])
    part = jnp.sum(part.reshape(BLOCKS, FORC, 128), axis=0)
    prev_ref[...] = part[:, 0:4]
    own_ref[...] = part[:, 4:8]
    next_ref[...] = part[:, 8:12]


def unpack(back, shapes, hot):
    part = jax.ShapeDtypeStruct((FORC, 4), F32)
    return pl.pallas_call(
        unpack_kernel,
        out_shape=(jax.ShapeDtypeStruct((ROWS, DOF), BF), part, part, part),
        scratch_shapes=[pltpu.VMEM((ROWS, WIDE), BF)],
        compiler_params=pltpu.CompilerParams(vmem_limit_bytes=32 * 1024 * 1024),
        name="unpack",
    )(back, shapes, hot)


def stacked(matrices):
    rows = jnp.concatenate(
        [m[:MAIN] for m in matrices] + [m[MAIN:] for m in matrices] + [jnp.zeros((64, DOF), BF)], axis=0
    )
    return jnp.concatenate([rows, rows[:, MAIN:]], axis=1)


def body(state, bits, couplings, shapes, amap):
    n_h, n_rad = lax.axis_size("h"), lax.axis_size("r")
    h, y, r = lax.axis_index("h"), lax.axis_index("y"), lax.axis_index("r")
    per_group = ACT // (n_h * RING * n_rad)
    ahead = [(i, i + 1) for i in range(n_h - 1)]
    back = [(b, a) for a, b in ahead]

    bits = jnp.pad(bits.reshape(BLOCKS, 4).astype(BF), ((0, 0), (DOF, WIDE - DOF - 4)))
    send = pack(state.reshape(ROWS, DOF), bits)
    mine = lax.all_to_all(send, ("y", "r"), 0, 0, tiled=True)
    reach = HALO // AXB * n_rad
    low = lax.ppermute(mine[-reach:], "h", ahead)
    high = lax.ppermute(mine[:reach], "h", back)

    fore = stacked([couplings[e] for e in range(5)])
    adj = stacked([couplings[e].T for e in (0, 2, 1, 4, 3)])
    out = steps(low, mine, high, fore, adj)
    back_home = lax.all_to_all(out, ("y", "r"), 0, 0, tiled=True)

    amap = amap.reshape(BLOCKS, 1)
    shift = (amap // per_group - ((h * RING + y) * n_rad + r)) // n_rad
    column = (shift + 1) * per_group + amap % per_group
    hot = (column == jnp.arange(128, dtype=jnp.int32)[None, :]).astype(BF)
    result, to_prev, own, to_next = unpack(back_home, shapes.reshape(BLOCKS, DOF), hot)
    n_ax = n_h * RING
    up = [(i, i + 1) for i in range(n_ax - 1)]
    from_prev = lax.ppermute(to_next, ("h", "y"), up)
    from_next = lax.ppermute(to_prev, ("h", "y"), [(b, a) for a, b in up])
    return result.reshape(state.shape), own + from_prev + from_next


def solution(mesh):
    n_ax, n_rad = mesh.shape["ax"], mesh.shape["rad"]
    fine = Mesh(mesh.devices.reshape(n_ax // RING, RING, n_rad), ("h", "y", "r"))
    ax = ("h", "y")
    in_specs = (P(ax, "r"), P(ax, "r"), P(), P(ax, "r"), P(ax, "r"))
    out_specs = (P(ax, "r"), P(None, ("h", "y", "r")))
    return jax.shard_map(body, mesh=fine, in_specs=in_specs, out_specs=out_specs, check_vma=False)
```

```python
import jax
import jax.numpy as jnp
from jax import lax
from jax.experimental import pallas as pl
from jax.experimental.pallas import tpu as pltpu
from jax.sharding import Mesh, PartitionSpec as P

ACT = 4096
STEPS = 2
DOF = 320
FORC = 16
RING = 4
AXB = 2
RADB = 16
BLOCKS = AXB * RADB
WIDE = 384
MAIN = 256
HALO = 2 * STEPS
BF = jnp.bfloat16
F32 = jnp.float32
ROWS = FORC * BLOCKS
NRAD = 4
LINE = NRAD * RADB
WINDOW = RING * AXB + 2 * HALO
DEPTH = 5 * MAIN + WIDE
PACKED = 80


def iota(shape, dim):
    return lax.broadcasted_iota(jnp.int32, shape, dim)


def one_hot(rows, cols, of_row):
    return jnp.where(iota((rows, cols), 1) == of_row(iota((rows, cols), 0)), 1.0, 0.0).astype(BF)


def dot(a, b):
    return jnp.dot(a, b, preferred_element_type=F32)


def dot_nt(a, b):
    return lax.dot_general(a, b, (((1,), (1,)), ((), ())), preferred_element_type=F32)


def call(kernel, out_shape, scratch_shapes, name, mib, flops, in_specs=None):
    return pl.pallas_call(
        kernel,
        out_shape=out_shape,
        **({} if in_specs is None else {"in_specs": in_specs}),
        scratch_shapes=scratch_shapes,
        compiler_params=pltpu.CompilerParams(vmem_limit_bytes=mib * 1024 * 1024),
        cost_estimate=pl.CostEstimate(flops=flops, bytes_accessed=2 * 1024 * 1024, transcendentals=0),
        name=name,
    )


def pack_kernel(state_ref, bits_ref, out_ref, rows, wide, bits, sem):
    copy = pltpu.make_async_copy(state_ref, rows, sem)
    copy.start()
    order = one_hot(ROWS, ROWS, lambda o: (o % BLOCKS) * FORC + o // BLOCKS)
    bits[...] = jnp.zeros_like(bits)
    for a in range(AXB):
        bits[a, 64:68, :RADB] = bits_ref[a].astype(F32)
    spread = [dot_nt(one_hot(ROWS, 128, lambda o: o % BLOCKS - a * RADB), bits[a].astype(BF)) for a in range(AXB)]
    wide[:, MAIN:] = jnp.zeros((ROWS, 128), BF)
    copy.wait()
    wide[:, :DOF] = rows[...]
    out = dot(order, wide[...]).astype(BF)
    meta = (spread[0] + spread[1]).astype(BF)
    out_ref[:, :, :MAIN] = out[:, :MAIN].reshape(FORC, BLOCKS, MAIN)
    out_ref[:, :, MAIN:] = (out[:, MAIN:] + meta).reshape(FORC, BLOCKS, 128)


def pack(state, bits):
    return call(
        pack_kernel,
        jax.ShapeDtypeStruct((FORC, BLOCKS, WIDE), BF),
        [pltpu.VMEM((ROWS, DOF), BF), pltpu.VMEM((ROWS, WIDE), BF), pltpu.VMEM((AXB, 128, 128), F32), pltpu.SemaphoreType.DMA],
        "pack",
        16,
        2 * ROWS * ROWS * WIDE,
        [pl.BlockSpec(memory_space=pl.ANY), pl.BlockSpec(memory_space=pltpu.VMEM)],
    )(state, bits)


def weights_kernel(couplings_ref, fore_ref, adj_ref):
    twice = jnp.where(
        (iota((DOF, WIDE), 1) == iota((DOF, WIDE), 0)) | (iota((DOF, WIDE), 1) == iota((DOF, WIDE), 0) + 64)
        & (iota((DOF, WIDE), 1) >= DOF),
        1.0,
        0.0,
    ).astype(BF)
    same = one_hot(DOF, DOF, lambda o: o)

    def put(ref, at, value):
        ref[at * MAIN : (at + 1) * MAIN, :] = value[:MAIN].astype(BF)
        ref[5 * MAIN + at * 64 : 5 * MAIN + (at + 1) * 64, :] = value[MAIN:].astype(BF)

    for at in range(5):
        put(fore_ref, at, dot(couplings_ref[at], twice))
    for at, e in enumerate((0, 2, 1, 4, 3)):
        matrix = couplings_ref[e]
        put(adj_ref, at, dot_nt(same, jnp.concatenate([matrix, matrix[MAIN:]], axis=0)))
    for ref in (fore_ref, adj_ref):
        ref[DEPTH - 64 :, :] = jnp.zeros((64, WIDE), BF)


def make_weights(couplings):
    shape = jax.ShapeDtypeStruct((DEPTH, WIDE), BF)
    return call(weights_kernel, (shape, shape), [], "weights", 16, 2 * 10 * DOF * DOF * WIDE)(couplings)


def put_rows(ref, row, source, slot, half):
    for r in range(NRAD):
        ref[row * LINE + r * RADB : row * LINE + (r + 1) * RADB, :] = source[slot + r, half * RADB : (half + 1) * RADB, :]


def spread_bits(field, masks, first, last):
    a, b = first * LINE, last * LINE
    pick = jnp.where(iota((128, 512), 0) == 64 + iota((128, 512), 1) // 128, 1.0, 0.0).astype(BF)
    tail = field[a:b, MAIN:]
    spread = dot(tail, pick)
    place = iota((b - a, 128), 0) % LINE
    masks[a:b, :256] = spread[:, :256].astype(BF)
    masks[a:b, 256:384] = jnp.where(place > 0, spread[:, 256:384], 0.0).astype(BF)
    masks[a:b, 384:] = jnp.where(place < LINE - 1, spread[:, 384:], 0.0).astype(BF)
    tail = tail.astype(F32)
    tail = jnp.where(iota((b - a, 128), 1) < 64, tail, pltpu.roll(tail, 64, 1))
    field[a:b, MAIN:] = tail.astype(BF)


def sides(value, masks, left, right, first, last):
    a, b = first * LINE, last * LINE
    down, up = pltpu.roll(value, 1, 0).astype(BF), pltpu.roll(value, b - a - 1, 0).astype(BF)
    for t in range(3):
        cols = slice(128 * t, 128 * t + 128)
        left[a:b, cols] = down[:, cols] * masks[a:b, 256:384]
        right[a:b, cols] = up[:, cols] * masks[a:b, 384:]


def stencil(field, masks, left, right, weights, first, last):
    a, b = first * LINE, last * LINE
    first_half = iota((b - a, 128), 1) < 64
    m0, m1 = masks[a:b, :128], masks[a:b, 128:256]
    prev, own, nxt = field[a - LINE : b - LINE, :], field[a:b, :], field[a + LINE : b + LINE, :]
    lhs = jnp.concatenate(
        [
            own[:, :MAIN],
            prev[:, :128] * m0,
            prev[:, 128:256] * m0,
            nxt[:, :128] * m1,
            nxt[:, 128:256] * m1,
            left[a:b, :MAIN],
            right[a:b, :MAIN],
            jnp.where(first_half, own[:, MAIN:], prev[:, MAIN:] * m0),
            jnp.where(first_half, nxt[:, MAIN:] * m1, left[a:b, MAIN:]),
            right[a:b, MAIN:],
        ],
        axis=1,
    )
    return dot(lhs, weights[...])


KEEP = []
for level in range(4):
    lo, hi = HALO + level, WINDOW - HALO - 1 - level
    edge = [lo, lo + 1, hi - 1, hi] if level < 3 else [lo, hi]
    KEEP += [(0, level, row) for row in edge]
    KEEP += [(side, level, row) for side in (1, 2) for row in (lo, hi)]
INNER = WINDOW - 2 * HALO


def inner_kernel(mine_ref, fore_ref, adj_ref, keep_ref, mask_ref, s_a, s_b, left, right):
    for i in range(INNER):
        put_rows(s_a, i, mine_ref, (i // AXB) * NRAD, i % AXB)
    spread_bits(s_a, mask_ref, 0, INNER)
    sides(s_a[...].astype(F32), mask_ref, left, right, 0, INNER)

    def keep(level, field):
        for at, (kind, of, row) in enumerate(KEEP):
            if of == level:
                a = (row - HALO) * LINE
                keep_ref[at * LINE : (at + 1) * LINE, :] = (field, left, right)[kind][a : a + LINE, :]

    keep(0, s_a)
    now, later = s_a, s_b
    for level in range(1, 4):
        first, last = level, INNER - level
        value = stencil(now, mask_ref, left, right, fore_ref if level <= STEPS else adj_ref, first, last)
        later[first * LINE : last * LINE, :] = value.astype(BF)
        sides(value, mask_ref, left, right, first, last)
        keep(level, later)
        now, later = later, now


def inner(mine, fore, adj):
    field = pltpu.VMEM((INNER * LINE, WIDE), BF)
    return call(
        inner_kernel,
        (jax.ShapeDtypeStruct((len(KEEP) * LINE, WIDE), BF), jax.ShapeDtypeStruct((INNER * LINE, 512), BF)),
        [field, field, field, field],
        "inner",
        24,
        2 * 12 * LINE * DEPTH * WIDE,
    )(mine, fore, adj)


def outer_kernel(low_ref, high_ref, keep_ref, mask_ref, fore_ref, adj_ref, out_ref, s_a, s_b, left, right, masks):
    for i in range(HALO):
        put_rows(s_a, i, low_ref, (i // AXB) * NRAD, i % AXB)
        put_rows(s_a, WINDOW - HALO + i, high_ref, (i // AXB) * NRAD, i % AXB)
    masks[HALO * LINE : (WINDOW - HALO) * LINE, :] = mask_ref[...]
    for first, last in ((0, HALO), (WINDOW - HALO, WINDOW)):
        spread_bits(s_a, masks, first, last)
        sides(s_a[first * LINE : last * LINE, :].astype(F32), masks, left, right, first, last)

    now, later = s_a, s_b
    for level in range(4):
        for at, (kind, of, row) in enumerate(KEEP):
            if of == level:
                (now, left, right)[kind][row * LINE : (row + 1) * LINE, :] = keep_ref[at * LINE : (at + 1) * LINE, :]
        for first in (level + 1, WINDOW - HALO - 1 - level):
            last = first + HALO
            value = stencil(now, masks, left, right, fore_ref if level < STEPS else adj_ref, first, last)
            later[first * LINE : last * LINE, :] = value.astype(BF)
            if level < 3:
                sides(value, masks, left, right, first, last)
        now, later = later, now

    early = iota((RADB, 128), 1) < 64
    for y in range(RING):
        for r in range(NRAD):
            rows = [(HALO + y * AXB + half) * LINE + r * RADB for half in range(AXB)]
            slot = y * NRAD + r
            for half, row in enumerate(rows):
                out_ref[slot, half * RADB : (half + 1) * RADB, :] = now[row : row + RADB, :128]
                out_ref[slot, BLOCKS + half * RADB : BLOCKS + (half + 1) * RADB, :] = now[row : row + RADB, 128:256]
            out_ref[slot, 2 * BLOCKS :, :] = jnp.where(early, now[rows[0] : rows[0] + RADB, MAIN:], now[rows[1] : rows[1] + RADB, MAIN:])


def outer(low, high, keep, masks, fore, adj):
    field = pltpu.VMEM((WINDOW * LINE, WIDE), BF)
    return call(
        outer_kernel,
        jax.ShapeDtypeStruct((FORC, PACKED, 128), BF),
        [field, field, field, field, pltpu.VMEM((WINDOW * LINE, 512), BF)],
        "outer",
        24,
        2 * 32 * LINE * DEPTH * WIDE,
    )(low, high, keep, masks, fore, adj)


def project_kernel(back_ref, shapes_ref, column_ref, prev_ref, own_ref, next_ref):
    shapes = shapes_ref[...].astype(F32)
    tails = jnp.concatenate([shapes[:RADB, MAIN:], shapes[RADB:, MAIN:]], axis=1)
    back = back_ref[...].astype(F32)
    body_sum = back[:, :BLOCKS] * shapes[None, :, :128] + back[:, BLOCKS : 2 * BLOCKS] * shapes[None, :, 128:256]
    tail = back[:, 2 * BLOCKS :] * tails[None]
    early = iota((FORC, RADB, 128), 2) < 64
    tail = jnp.concatenate([jnp.where(early, tail, 0.0), jnp.where(early, 0.0, tail)], axis=1)
    proj = jnp.sum(body_sum + tail, axis=2, keepdims=True)
    lane = iota((BLOCKS, 128), 1)
    by_block = jnp.zeros((BLOCKS, 128), F32)
    for f in range(FORC):
        by_block = jnp.where(lane == f, proj[f], by_block)
    column = column_ref[...]
    for at, ref in enumerate((prev_ref, own_ref, next_ref)):
        for slot in range(4):
            part = jnp.sum(jnp.where(column == 4 * at + slot, by_block, 0.0), axis=0, keepdims=True)
            ref[slot : slot + 1, :] = part[:, :FORC]


def project(back, shapes, column):
    part = jax.ShapeDtypeStruct((4, FORC), F32)
    return call(project_kernel, (part, part, part), [], "project", 16, 2 * ROWS * DOF)(back, shapes, column)


def place_kernel(back_ref, state_ref, wide):
    for f in range(FORC):
        row = f * BLOCKS
        wide[row : row + BLOCKS, :128] = back_ref[f, :BLOCKS, :]
        wide[row : row + BLOCKS, 128:256] = back_ref[f, BLOCKS : 2 * BLOCKS, :]
        tail = back_ref[f, 2 * BLOCKS :, :]
        wide[row : row + RADB, MAIN:] = tail
        wide[row + RADB : row + BLOCKS, MAIN:] = pltpu.roll(tail.astype(F32), 64, 1).astype(BF)
    order = one_hot(ROWS, ROWS, lambda o: (o % FORC) * BLOCKS + o // FORC)
    state_ref[...] = dot(order, wide[...])[:, :DOF].astype(BF)


def place(back):
    return call(
        place_kernel, jax.ShapeDtypeStruct((ROWS, DOF), BF), [pltpu.VMEM((ROWS, WIDE), BF)], "place", 16, 2 * ROWS * ROWS * WIDE
    )(back)


def body(state, bits, couplings, shapes, amap):
    n_h, n_rad = lax.axis_size("h"), lax.axis_size("r")
    h, y, r = lax.axis_index("h"), lax.axis_index("y"), lax.axis_index("r")
    per_group = ACT // (n_h * RING * n_rad)
    ahead = [(i, i + 1) for i in range(n_h - 1)]
    back = [(b, a) for a, b in ahead]

    send = pack(state.reshape(ROWS, DOF), bits.transpose(0, 2, 1))
    mine = lax.all_to_all(send, ("y", "r"), 0, 0, tiled=True)
    fore, adj = make_weights(couplings)
    reach = HALO // AXB * n_rad
    low = lax.ppermute(mine[-reach:], "h", ahead)
    high = lax.ppermute(mine[:reach], "h", back)
    keep, masks = inner(mine, fore, adj)
    out = outer(low, high, keep, masks, fore, adj)
    back_home = lax.all_to_all(out, ("y", "r"), 0, 0, tiled=True)

    amap = amap.reshape(BLOCKS, 1)
    shift = (amap // per_group - ((h * RING + y) * n_rad + r)) // n_rad
    column = (shift + 1) * per_group + amap % per_group
    to_prev, own, to_next = project(back_home, shapes.reshape(BLOCKS, DOF), column)
    n_ax = n_h * RING
    up = [(i, i + 1) for i in range(n_ax - 1)]
    from_prev = lax.ppermute(to_next, ("h", "y"), up)
    from_next = lax.ppermute(to_prev, ("h", "y"), [(b, a) for a, b in up])
    result = place(back_home)
    return result.reshape(state.shape), (own + from_prev + from_next).T


def solution(mesh):
    n_ax, n_rad = mesh.shape["ax"], mesh.shape["rad"]
    fine = Mesh(mesh.devices.reshape(n_ax // RING, RING, n_rad), ("h", "y", "r"))
    ax = ("h", "y")
    in_specs = (P(ax, "r"), P(ax, "r"), P(), P(ax, "r"), P(ax, "r"))
    out_specs = (P(ax, "r"), P(None, ("h", "y", "r")))
    return jax.shard_map(body, mesh=fine, in_specs=in_specs, out_specs=out_specs, check_vma=False)
```

```python
import functools

import jax
import jax.numpy as jnp
from jax import lax
from jax.experimental import pallas as pl
from jax.experimental.pallas import tpu as pltpu
from jax.sharding import Mesh, PartitionSpec as P

ACT = 4096
STEPS = 2
DOF = 320
FORC = 16
RING = 4
AXB = 2
RADB = 16
BLOCKS = AXB * RADB
WIDE = 384
MAIN = 256
HALO = 2 * STEPS
BF = jnp.bfloat16
F32 = jnp.float32
ROWS = FORC * BLOCKS
NRAD = 4
LINE = NRAD * RADB
WINDOW = RING * AXB + 2 * HALO
DEPTH = 5 * MAIN + WIDE
PACKED = 80


def iota(shape, dim):
    return lax.broadcasted_iota(jnp.int32, shape, dim)


def one_hot(rows, cols, of_row):
    return jnp.where(iota((rows, cols), 1) == of_row(iota((rows, cols), 0)), 1.0, 0.0).astype(BF)


def dot(a, b):
    return jnp.dot(a, b, preferred_element_type=F32)


def dot_nt(a, b):
    return lax.dot_general(a, b, (((1,), (1,)), ((), ())), preferred_element_type=F32)


def call(kernel, out_shape, scratch_shapes, name, mib, flops, in_specs=None):
    return pl.pallas_call(
        kernel,
        out_shape=out_shape,
        **({} if in_specs is None else {"in_specs": in_specs}),
        scratch_shapes=scratch_shapes,
        compiler_params=pltpu.CompilerParams(vmem_limit_bytes=mib * 1024 * 1024),
        cost_estimate=pl.CostEstimate(flops=flops, bytes_accessed=2 * 1024 * 1024, transcendentals=0),
        name=name,
    )


def pack_kernel(state_ref, bits_ref, out_ref, rows, links, wide, bits, sems):
    copy = pltpu.make_async_copy(state_ref, rows, sems.at[0])
    link_copy = pltpu.make_async_copy(bits_ref, links, sems.at[1])
    link_copy.start()
    copy.start()
    order = one_hot(ROWS, ROWS, lambda o: (o % BLOCKS) * FORC + o // BLOCKS)
    bits[...] = jnp.zeros_like(bits)
    wide[:, MAIN:] = jnp.zeros((ROWS, 128), BF)
    link_copy.wait()
    for a in range(AXB):
        bits[a, 64:68, :RADB] = links[a].astype(F32)
    spread = [dot_nt(one_hot(ROWS, 128, lambda o: o % BLOCKS - a * RADB), bits[a].astype(BF)) for a in range(AXB)]
    copy.wait()
    wide[:, :DOF] = rows[...]
    out = dot(order, wide[...]).astype(BF)
    meta = (spread[0] + spread[1]).astype(BF)
    out_ref[:, :, :MAIN] = out[:, :MAIN].reshape(FORC, BLOCKS, MAIN)
    out_ref[:, :, MAIN:] = (out[:, MAIN:] + meta).reshape(FORC, BLOCKS, 128)


def pack(state, bits):
    return call(
        pack_kernel,
        jax.ShapeDtypeStruct((FORC, BLOCKS, WIDE), BF),
        [
            pltpu.VMEM((ROWS, DOF), BF),
            pltpu.VMEM((AXB, 4, RADB), jnp.int32),
            pltpu.VMEM((ROWS, WIDE), BF),
            pltpu.VMEM((AXB, 128, 128), F32),
            pltpu.SemaphoreType.DMA((2,)),
        ],
        "pack",
        16,
        2 * ROWS * ROWS * WIDE,
        [pl.BlockSpec(memory_space=pltpu.HBM)] * 2,
    )(state, bits)


def stack_weights(couplings_ref, fore_ref, adj_ref):
    twice = jnp.where(
        (iota((DOF, WIDE), 1) == iota((DOF, WIDE), 0)) | (iota((DOF, WIDE), 1) == iota((DOF, WIDE), 0) + 64)
        & (iota((DOF, WIDE), 1) >= DOF),
        1.0,
        0.0,
    ).astype(BF)
    same = one_hot(DOF, DOF, lambda o: o)

    def put(ref, at, value):
        ref[at * MAIN : (at + 1) * MAIN, :] = value[:MAIN].astype(BF)
        ref[5 * MAIN + at * 64 : 5 * MAIN + (at + 1) * 64, :] = value[MAIN:].astype(BF)

    for at in range(5):
        put(fore_ref, at, dot(couplings_ref[at], twice))
    for at, e in enumerate((0, 2, 1, 4, 3)):
        matrix = couplings_ref[e]
        put(adj_ref, at, dot_nt(same, jnp.concatenate([matrix, matrix[MAIN:]], axis=0)))
    for ref in (fore_ref, adj_ref):
        ref[DEPTH - 64 :, :] = jnp.zeros((64, WIDE), BF)


def put_rows(ref, row, source, slot, half):
    for r in range(NRAD):
        ref[row * LINE + r * RADB : row * LINE + (r + 1) * RADB, :] = source[slot + r, half * RADB : (half + 1) * RADB, :]


def spread_bits(field, masks, first, last):
    a, b = first * LINE, last * LINE
    pick = jnp.where(iota((128, 512), 0) == 64 + iota((128, 512), 1) // 128, 1.0, 0.0).astype(BF)
    tail = field[a:b, MAIN:]
    spread = dot(tail, pick)
    place = iota((b - a, 128), 0) % LINE
    masks[a:b, :256] = spread[:, :256].astype(BF)
    masks[a:b, 256:384] = jnp.where(place > 0, spread[:, 256:384], 0.0).astype(BF)
    masks[a:b, 384:] = jnp.where(place < LINE - 1, spread[:, 384:], 0.0).astype(BF)
    tail = tail.astype(F32)
    tail = jnp.where(iota((b - a, 128), 1) < 64, tail, pltpu.roll(tail, 64, 1))
    field[a:b, MAIN:] = tail.astype(BF)


def sides(value, masks, left, right, first, last):
    a, b = first * LINE, last * LINE
    down, up = pltpu.roll(value, 1, 0).astype(BF), pltpu.roll(value, b - a - 1, 0).astype(BF)
    for t in range(3):
        cols = slice(128 * t, 128 * t + 128)
        left[a:b, cols] = down[:, cols] * masks[a:b, 256:384]
        right[a:b, cols] = up[:, cols] * masks[a:b, 384:]


def stencil(field, masks, left, right, weights, first, last):
    a, b = first * LINE, last * LINE
    first_half = iota((b - a, 128), 1) < 64
    m0, m1 = masks[a:b, :128], masks[a:b, 128:256]
    prev, own, nxt = field[a - LINE : b - LINE, :], field[a:b, :], field[a + LINE : b + LINE, :]
    lhs = jnp.concatenate(
        [
            own[:, :MAIN],
            prev[:, :128] * m0,
            prev[:, 128:256] * m0,
            nxt[:, :128] * m1,
            nxt[:, 128:256] * m1,
            left[a:b, :MAIN],
            right[a:b, :MAIN],
            jnp.where(first_half, own[:, MAIN:], prev[:, MAIN:] * m0),
            jnp.where(first_half, nxt[:, MAIN:] * m1, left[a:b, MAIN:]),
            right[a:b, MAIN:],
        ],
        axis=1,
    )
    return dot(lhs, weights[...])


KEEP = []
for level in range(4):
    lo, hi = HALO + level, WINDOW - HALO - 1 - level
    edge = [lo, lo + 1, hi - 1, hi] if level < 3 else [lo, hi]
    KEEP += [(0, level, row) for row in edge]
    KEEP += [(side, level, row) for side in (1, 2) for row in (lo, hi)]
INNER = WINDOW - 2 * HALO


def inner_kernel(mine_ref, couplings_ref, fore_ref, adj_ref, keep_ref, mask_ref, s_a, s_b, left, right):
    stack_weights(couplings_ref, fore_ref, adj_ref)
    for i in range(INNER):
        put_rows(s_a, i, mine_ref, (i // AXB) * NRAD, i % AXB)
    spread_bits(s_a, mask_ref, 0, INNER)
    sides(s_a[...].astype(F32), mask_ref, left, right, 0, INNER)

    def keep(level, field):
        for at, (kind, of, row) in enumerate(KEEP):
            if of == level:
                a = (row - HALO) * LINE
                keep_ref[at * LINE : (at + 1) * LINE, :] = (field, left, right)[kind][a : a + LINE, :]

    keep(0, s_a)
    now, later = s_a, s_b
    for level in range(1, 4):
        first, last = level, INNER - level
        value = stencil(now, mask_ref, left, right, fore_ref if level <= STEPS else adj_ref, first, last)
        later[first * LINE : last * LINE, :] = value.astype(BF)
        sides(value, mask_ref, left, right, first, last)
        keep(level, later)
        now, later = later, now


def inner(mine, couplings):
    field = pltpu.VMEM((INNER * LINE, WIDE), BF)
    weights = jax.ShapeDtypeStruct((DEPTH, WIDE), BF)
    return call(
        inner_kernel,
        (weights, weights, jax.ShapeDtypeStruct((len(KEEP) * LINE, WIDE), BF), jax.ShapeDtypeStruct((INNER * LINE, 512), BF)),
        [field, field, field, field],
        "inner",
        24,
        2 * 12 * LINE * DEPTH * WIDE,
    )(mine, couplings)


def outer_kernel(upper, *refs):
    halo_ref, keep_ref, mask_ref, fore_ref, adj_ref = refs[:5]
    out_ref, s_a, s_b, left, right, masks = refs[-6:]
    edge = WINDOW - HALO if upper else 0
    for i in range(HALO):
        put_rows(s_a, edge + i, halo_ref, (i // AXB) * NRAD, i % AXB)
    half = WINDOW // 2 if upper else HALO
    at = (half - HALO) * LINE
    masks[half * LINE : (half + HALO) * LINE, :] = mask_ref[at : at + HALO * LINE, :]
    spread_bits(s_a, masks, edge, edge + HALO)
    sides(s_a[edge * LINE : (edge + HALO) * LINE, :].astype(F32), masks, left, right, edge, edge + HALO)

    now, later = s_a, s_b
    for level in range(4):
        for at, (kind, of, row) in enumerate(KEEP):
            if of == level:
                (now, left, right)[kind][row * LINE : (row + 1) * LINE, :] = keep_ref[at * LINE : (at + 1) * LINE, :]
        first = WINDOW - HALO - 1 - level if upper else level + 1
        last = first + HALO
        value = stencil(now, masks, left, right, fore_ref if level < STEPS else adj_ref, first, last)
        later[first * LINE : last * LINE, :] = value.astype(BF)
        if level < 3:
            sides(value, masks, left, right, first, last)
        now, later = later, now

    early = iota((RADB, 128), 1) < 64
    slots = FORC // 2
    if upper:
        out_ref[:slots] = refs[5][...]
    for slot in range(slots):
        y, r = slot // NRAD, slot % NRAD
        rows = [(half + y * AXB + a) * LINE + r * RADB for a in range(AXB)]
        to = slot + (slots if upper else 0)
        for a, row in enumerate(rows):
            out_ref[to, a * RADB : (a + 1) * RADB, :] = now[row : row + RADB, :128]
            out_ref[to, BLOCKS + a * RADB : BLOCKS + (a + 1) * RADB, :] = now[row : row + RADB, 128:256]
        out_ref[to, 2 * BLOCKS :, :] = jnp.where(early, now[rows[0] : rows[0] + RADB, MAIN:], now[rows[1] : rows[1] + RADB, MAIN:])


def outer(upper, *args):
    field = pltpu.VMEM((WINDOW * LINE, WIDE), BF)
    return call(
        functools.partial(outer_kernel, upper),
        jax.ShapeDtypeStruct((FORC if upper else FORC // 2, PACKED, 128), BF),
        [field, field, field, field, pltpu.VMEM((WINDOW * LINE, 512), BF)],
        "upper" if upper else "lower",
        24,
        2 * 16 * LINE * DEPTH * WIDE,
    )(*args)


def project_kernel(back_ref, shapes_ref, column_ref, prev_ref, own_ref, next_ref):
    shapes = shapes_ref[...].astype(F32)
    tails = jnp.concatenate([shapes[:RADB, MAIN:], shapes[RADB:, MAIN:]], axis=1)
    back = back_ref[...].astype(F32)
    body_sum = back[:, :BLOCKS] * shapes[None, :, :128] + back[:, BLOCKS : 2 * BLOCKS] * shapes[None, :, 128:256]
    tail = back[:, 2 * BLOCKS :] * tails[None]
    early = iota((FORC, RADB, 128), 2) < 64
    tail = jnp.concatenate([jnp.where(early, tail, 0.0), jnp.where(early, 0.0, tail)], axis=1)
    proj = jnp.sum(body_sum + tail, axis=2, keepdims=True)
    lane = iota((BLOCKS, 128), 1)
    by_block = jnp.zeros((BLOCKS, 128), F32)
    for f in range(FORC):
        by_block = jnp.where(lane == f, proj[f], by_block)
    column = column_ref[...]
    for at, ref in enumerate((prev_ref, own_ref, next_ref)):
        for slot in range(4):
            part = jnp.sum(jnp.where(column == 4 * at + slot, by_block, 0.0), axis=0, keepdims=True)
            ref[slot : slot + 1, :] = part[:, :FORC]


def project(back, shapes, column):
    part = jax.ShapeDtypeStruct((4, FORC), F32)
    return call(project_kernel, (part, part, part), [], "project", 16, 2 * ROWS * DOF)(back, shapes, column)


def place_kernel(back_ref, state_ref, wide):
    for f in range(FORC):
        row = f * BLOCKS
        wide[row : row + BLOCKS, :128] = back_ref[f, :BLOCKS, :]
        wide[row : row + BLOCKS, 128:256] = back_ref[f, BLOCKS : 2 * BLOCKS, :]
        tail = back_ref[f, 2 * BLOCKS :, :]
        wide[row : row + RADB, MAIN:] = tail
        wide[row + RADB : row + BLOCKS, MAIN:] = pltpu.roll(tail.astype(F32), 64, 1).astype(BF)
    order = one_hot(ROWS, ROWS, lambda o: (o % FORC) * BLOCKS + o // FORC)
    state_ref[...] = dot(order, wide[...])[:, :DOF].astype(BF)


def place(back):
    return call(
        place_kernel, jax.ShapeDtypeStruct((ROWS, DOF), BF), [pltpu.VMEM((ROWS, WIDE), BF)], "place", 16, 2 * ROWS * ROWS * WIDE
    )(back)


def swaps(firsts):
    return [pair for i in firsts for pair in ((i, i + 1), (i + 1, i))]


def body(state, bits, couplings, shapes, amap):
    n_h, n_rad = lax.axis_size("h"), lax.axis_size("r")
    h, y, r = lax.axis_index("h"), lax.axis_index("y"), lax.axis_index("r")
    per_group = ACT // (n_h * RING * n_rad)
    ahead = [(i, i + 1) for i in range(n_h - 1)]
    back = [(b, a) for a, b in ahead]

    send = pack(state.reshape(ROWS, DOF), bits.transpose(0, 2, 1))
    mine = lax.all_to_all(send, ("y", "r"), 0, 0, tiled=True)
    reach = HALO // AXB * n_rad
    low = lax.ppermute(mine[-reach:], "h", ahead)
    high = lax.ppermute(mine[:reach], "h", back)
    amap = amap.reshape(BLOCKS, 1)
    shift = (amap // per_group - ((h * RING + y) * n_rad + r)) // n_rad
    column = (shift + 1) * per_group + amap % per_group
    mine, column = lax.optimization_barrier((mine, column))
    fore, adj, keep, masks = inner(mine, couplings)
    lower = outer(False, low, keep, masks, fore, adj)
    out = outer(True, high, keep, masks, fore, adj, lower)
    back_home = lax.all_to_all(out, ("y", "r"), 0, 0, tiled=True)

    to_prev, own, to_next = project(back_home, shapes.reshape(BLOCKS, DOF), column)
    n_ax = n_h * RING
    far = swaps(range(1, n_ax - 1, 2))
    near = swaps(range(0, n_ax - 1, 2))
    odd = y % 2 == 1
    from_far = lax.ppermute(jnp.where(odd, to_next, to_prev), ("h", "y"), far)
    from_near = lax.ppermute(jnp.where(odd, to_prev, to_next), ("h", "y"), near)
    result = place(back_home)
    return result.reshape(state.shape), (own + from_far + from_near).T


def solution(mesh):
    n_ax, n_rad = mesh.shape["ax"], mesh.shape["rad"]
    fine = Mesh(mesh.devices.reshape(n_ax // RING, RING, n_rad), ("h", "y", "r"))
    ax = ("h", "y")
    in_specs = (P(ax, "r"), P(ax, "r"), P(), P(ax, "r"), P(ax, "r"))
    out_specs = (P(ax, "r"), P(None, ("h", "y", "r")))
    return jax.shard_map(body, mesh=fine, in_specs=in_specs, out_specs=out_specs, check_vma=False)
```

```python
import functools

import jax
import jax.numpy as jnp
from jax import lax
from jax.experimental import pallas as pl
from jax.experimental.pallas import tpu as pltpu
from jax.sharding import Mesh, PartitionSpec as P

ACT = 4096
STEPS = 2
DOF = 320
FORC = 16
RING = 4
AXB = 2
RADB = 16
BLOCKS = AXB * RADB
WIDE = 384
MAIN = 256
HALO = 2 * STEPS
BF = jnp.bfloat16
F32 = jnp.float32
ROWS = FORC * BLOCKS
NRAD = 4
LINE = NRAD * RADB
WINDOW = RING * AXB + 2 * HALO
DEPTH = 5 * MAIN + WIDE
PACKED = 80


def iota(shape, dim):
    return lax.broadcasted_iota(jnp.int32, shape, dim)


def one_hot(rows, cols, of_row):
    return jnp.where(iota((rows, cols), 1) == of_row(iota((rows, cols), 0)), 1.0, 0.0).astype(BF)


def dot(a, b):
    return jnp.dot(a, b, preferred_element_type=F32)


def dot_nt(a, b):
    return lax.dot_general(a, b, (((1,), (1,)), ((), ())), preferred_element_type=F32)


def call(kernel, out_shape, scratch_shapes, name, mib, flops, in_specs=None):
    return pl.pallas_call(
        kernel,
        out_shape=out_shape,
        **({} if in_specs is None else {"in_specs": in_specs}),
        scratch_shapes=scratch_shapes,
        compiler_params=pltpu.CompilerParams(vmem_limit_bytes=mib * 1024 * 1024),
        cost_estimate=pl.CostEstimate(flops=flops, bytes_accessed=2 * 1024 * 1024, transcendentals=0),
        name=name,
    )


def pack_kernel(state_ref, bits_ref, out_ref, rows, links, wide, bits, sems):
    copy = pltpu.make_async_copy(state_ref, rows, sems.at[0])
    link_copy = pltpu.make_async_copy(bits_ref, links, sems.at[1])
    link_copy.start()
    copy.start()
    order = one_hot(ROWS, ROWS, lambda o: (o % BLOCKS) * FORC + o // BLOCKS)
    bits[...] = jnp.zeros_like(bits)
    wide[:, MAIN:] = jnp.zeros((ROWS, 128), BF)
    link_copy.wait()
    for a in range(AXB):
        bits[a, 64:68, :RADB] = links[a].astype(F32)
    spread = [dot_nt(one_hot(ROWS, 128, lambda o: o % BLOCKS - a * RADB), bits[a].astype(BF)) for a in range(AXB)]
    copy.wait()
    wide[:, :DOF] = rows[...]
    out = dot(order, wide[...]).astype(BF)
    meta = (spread[0] + spread[1]).astype(BF)
    out_ref[:, :, :MAIN] = out[:, :MAIN].reshape(FORC, BLOCKS, MAIN)
    out_ref[:, :, MAIN:] = (out[:, MAIN:] + meta).reshape(FORC, BLOCKS, 128)


def pack(state, bits):
    return call(
        pack_kernel,
        jax.ShapeDtypeStruct((FORC, BLOCKS, WIDE), BF),
        [
            pltpu.VMEM((ROWS, DOF), BF),
            pltpu.VMEM((AXB, 4, RADB), jnp.int32),
            pltpu.VMEM((ROWS, WIDE), BF),
            pltpu.VMEM((AXB, 128, 128), F32),
            pltpu.SemaphoreType.DMA((2,)),
        ],
        "pack",
        16,
        2 * ROWS * ROWS * WIDE,
        [pl.BlockSpec(memory_space=pltpu.HBM)] * 2,
    )(state, bits)


def stack_weights(couplings_ref, fore_ref, adj_ref):
    twice = jnp.where(
        (iota((DOF, WIDE), 1) == iota((DOF, WIDE), 0)) | (iota((DOF, WIDE), 1) == iota((DOF, WIDE), 0) + 64)
        & (iota((DOF, WIDE), 1) >= DOF),
        1.0,
        0.0,
    ).astype(BF)
    same = one_hot(DOF, DOF, lambda o: o)

    def put(ref, at, value):
        ref[at * MAIN : (at + 1) * MAIN, :] = value[:MAIN].astype(BF)
        ref[5 * MAIN + at * 64 : 5 * MAIN + (at + 1) * 64, :] = value[MAIN:].astype(BF)

    for at in range(5):
        put(fore_ref, at, dot(couplings_ref[at], twice))
    for at, e in enumerate((0, 2, 1, 4, 3)):
        matrix = couplings_ref[e]
        put(adj_ref, at, dot_nt(same, jnp.concatenate([matrix, matrix[MAIN:]], axis=0)))
    for ref in (fore_ref, adj_ref):
        ref[DEPTH - 64 :, :] = jnp.zeros((64, WIDE), BF)


def put_rows(ref, row, source, slot, half):
    for r in range(NRAD):
        ref[row * LINE + r * RADB : row * LINE + (r + 1) * RADB, :] = source[slot + r, half * RADB : (half + 1) * RADB, :]


def spread_bits(field, masks, first, last):
    a, b = first * LINE, last * LINE
    pick = jnp.where(iota((128, 512), 0) == 64 + iota((128, 512), 1) // 128, 1.0, 0.0).astype(BF)
    tail = field[a:b, MAIN:]
    spread = dot(tail, pick)
    place = iota((b - a, 128), 0) % LINE
    masks[a:b, :256] = spread[:, :256].astype(BF)
    masks[a:b, 256:384] = jnp.where(place > 0, spread[:, 256:384], 0.0).astype(BF)
    masks[a:b, 384:] = jnp.where(place < LINE - 1, spread[:, 384:], 0.0).astype(BF)
    tail = tail.astype(F32)
    tail = jnp.where(iota((b - a, 128), 1) < 64, tail, pltpu.roll(tail, 64, 1))
    field[a:b, MAIN:] = tail.astype(BF)


def sides(value, masks, left, right, first, last):
    a, b = first * LINE, last * LINE
    down, up = pltpu.roll(value, 1, 0).astype(BF), pltpu.roll(value, b - a - 1, 0).astype(BF)
    for t in range(3):
        cols = slice(128 * t, 128 * t + 128)
        left[a:b, cols] = down[:, cols] * masks[a:b, 256:384]
        right[a:b, cols] = up[:, cols] * masks[a:b, 384:]


def stencil(field, masks, left, right, weights, first, last):
    a, b = first * LINE, last * LINE
    first_half = iota((b - a, 128), 1) < 64
    m0, m1 = masks[a:b, :128], masks[a:b, 128:256]
    prev, own, nxt = field[a - LINE : b - LINE, :], field[a:b, :], field[a + LINE : b + LINE, :]
    lhs = jnp.concatenate(
        [
            own[:, :MAIN],
            prev[:, :128] * m0,
            prev[:, 128:256] * m0,
            nxt[:, :128] * m1,
            nxt[:, 128:256] * m1,
            left[a:b, :MAIN],
            right[a:b, :MAIN],
            jnp.where(first_half, own[:, MAIN:], prev[:, MAIN:] * m0),
            jnp.where(first_half, nxt[:, MAIN:] * m1, left[a:b, MAIN:]),
            right[a:b, MAIN:],
        ],
        axis=1,
    )
    return dot(lhs, weights[...])


KEEP = []
for level in range(4):
    lo, hi = HALO + level, WINDOW - HALO - 1 - level
    edge = [lo, lo + 1, hi - 1, hi] if level < 3 else [lo, hi]
    KEEP += [(0, level, row) for row in edge]
    KEEP += [(side, level, row) for side in (1, 2) for row in (lo, hi)]
INNER = WINDOW - 2 * HALO


def inner_kernel(mine_ref, couplings_ref, fore_ref, adj_ref, keep_ref, mask_ref, s_a, s_b, left, right):
    stack_weights(couplings_ref, fore_ref, adj_ref)
    for i in range(INNER):
        put_rows(s_a, i, mine_ref, (i // AXB) * NRAD, i % AXB)
    spread_bits(s_a, mask_ref, 0, INNER)
    sides(s_a[...].astype(F32), mask_ref, left, right, 0, INNER)

    def keep(level, field):
        for at, (kind, of, row) in enumerate(KEEP):
            if of == level:
                a = (row - HALO) * LINE
                keep_ref[at * LINE : (at + 1) * LINE, :] = (field, left, right)[kind][a : a + LINE, :]

    keep(0, s_a)
    now, later = s_a, s_b
    for level in range(1, 4):
        first, last = level, INNER - level
        value = stencil(now, mask_ref, left, right, fore_ref if level <= STEPS else adj_ref, first, last)
        later[first * LINE : last * LINE, :] = value.astype(BF)
        sides(value, mask_ref, left, right, first, last)
        keep(level, later)
        now, later = later, now


def inner(mine, couplings):
    field = pltpu.VMEM((INNER * LINE, WIDE), BF)
    weights = jax.ShapeDtypeStruct((DEPTH, WIDE), BF)
    return call(
        inner_kernel,
        (weights, weights, jax.ShapeDtypeStruct((len(KEEP) * LINE, WIDE), BF), jax.ShapeDtypeStruct((INNER * LINE, 512), BF)),
        [field, field, field, field],
        "inner",
        24,
        2 * 12 * LINE * DEPTH * WIDE,
    )(mine, couplings)


def outer_kernel(upper, *refs):
    halo_ref, keep_ref, mask_ref, fore_ref, adj_ref = refs[:5]
    out_ref, s_a, s_b, left, right, masks = refs[-6:]
    edge = WINDOW - HALO if upper else 0
    for i in range(HALO):
        put_rows(s_a, edge + i, halo_ref, (i // AXB) * NRAD, i % AXB)
    half = WINDOW // 2 if upper else HALO
    at = (half - HALO) * LINE
    masks[half * LINE : (half + HALO) * LINE, :] = mask_ref[at : at + HALO * LINE, :]
    spread_bits(s_a, masks, edge, edge + HALO)
    sides(s_a[edge * LINE : (edge + HALO) * LINE, :].astype(F32), masks, left, right, edge, edge + HALO)

    now, later = s_a, s_b
    for level in range(4):
        for at, (kind, of, row) in enumerate(KEEP):
            if of == level:
                (now, left, right)[kind][row * LINE : (row + 1) * LINE, :] = keep_ref[at * LINE : (at + 1) * LINE, :]
        first = WINDOW - HALO - 1 - level if upper else level + 1
        last = first + HALO
        value = stencil(now, masks, left, right, fore_ref if level < STEPS else adj_ref, first, last)
        later[first * LINE : last * LINE, :] = value.astype(BF)
        if level < 3:
            sides(value, masks, left, right, first, last)
        now, later = later, now

    early = iota((RADB, 128), 1) < 64
    slots = FORC // 2
    if upper:
        out_ref[:slots] = refs[5][...]
    for slot in range(slots):
        y, r = slot // NRAD, slot % NRAD
        rows = [(half + y * AXB + a) * LINE + r * RADB for a in range(AXB)]
        to = slot + (slots if upper else 0)
        for a, row in enumerate(rows):
            out_ref[to, a * RADB : (a + 1) * RADB, :] = now[row : row + RADB, :128]
            out_ref[to, BLOCKS + a * RADB : BLOCKS + (a + 1) * RADB, :] = now[row : row + RADB, 128:256]
        out_ref[to, 2 * BLOCKS :, :] = jnp.where(early, now[rows[0] : rows[0] + RADB, MAIN:], now[rows[1] : rows[1] + RADB, MAIN:])


def outer(upper, *args):
    field = pltpu.VMEM((WINDOW * LINE, WIDE), BF)
    return call(
        functools.partial(outer_kernel, upper),
        jax.ShapeDtypeStruct((FORC if upper else FORC // 2, PACKED, 128), BF),
        [field, field, field, field, pltpu.VMEM((WINDOW * LINE, 512), BF)],
        "upper" if upper else "lower",
        24,
        2 * 16 * LINE * DEPTH * WIDE,
    )(*args)


def project_kernel(back_ref, shapes_ref, map_ref, far_ref, near_ref, own_ref):
    y = lax.axis_index("y")
    group = (lax.axis_index("h") * RING + y) * NRAD + lax.axis_index("r")
    actuator = map_ref[...]
    column = (((((actuator >> 2) - group) >> 2) + 1) * 4 + (actuator & 3)).astype(F32)
    same = iota((RADB, RADB), 0) == iota((RADB, RADB), 1)
    column = jnp.concatenate(
        [jnp.sum(jnp.where(same, column[a : a + 1, :], 0.0), axis=1, keepdims=True) for a in range(AXB)], axis=0
    )
    shapes = shapes_ref[...].astype(F32)
    tails = jnp.concatenate([shapes[:RADB, MAIN:], shapes[RADB:, MAIN:]], axis=1)
    back = back_ref[...].astype(F32)
    body_sum = back[:, :BLOCKS] * shapes[None, :, :128] + back[:, BLOCKS : 2 * BLOCKS] * shapes[None, :, 128:256]
    tail = back[:, 2 * BLOCKS :] * tails[None]
    early = iota((FORC, RADB, 128), 2) < 64
    tail = jnp.concatenate([jnp.where(early, tail, 0.0), jnp.where(early, 0.0, tail)], axis=1)
    proj = jnp.sum(body_sum + tail, axis=2, keepdims=True)
    lane = iota((BLOCKS, 128), 1)
    by_block = jnp.zeros((BLOCKS, 128), F32)
    for f in range(FORC):
        by_block = jnp.where(lane == f, proj[f], by_block)
    parts = [
        [jnp.sum(jnp.where(column == 4 * at + slot, by_block, 0.0), axis=0, keepdims=True)[:, :FORC] for slot in range(4)]
        for at in range(3)
    ]
    odd = jnp.broadcast_to(y % 2, (1, FORC)) == 1
    for slot in range(4):
        to_prev, own, to_next = [part[slot] for part in parts]
        far_ref[slot : slot + 1, :] = jnp.where(odd, to_next, to_prev)
        near_ref[slot : slot + 1, :] = jnp.where(odd, to_prev, to_next)
        own_ref[slot : slot + 1, :] = own


def project(back, shapes, amap):
    part = jax.ShapeDtypeStruct((4, FORC), F32)
    return call(project_kernel, (part, part, part), [], "project", 16, 2 * ROWS * DOF)(back, shapes, amap)


def place_kernel(back_ref, state_ref, wide):
    for f in range(FORC):
        row = f * BLOCKS
        wide[row : row + BLOCKS, :128] = back_ref[f, :BLOCKS, :]
        wide[row : row + BLOCKS, 128:256] = back_ref[f, BLOCKS : 2 * BLOCKS, :]
        tail = back_ref[f, 2 * BLOCKS :, :]
        wide[row : row + RADB, MAIN:] = tail
        wide[row + RADB : row + BLOCKS, MAIN:] = pltpu.roll(tail.astype(F32), 64, 1).astype(BF)
    order = one_hot(ROWS, ROWS, lambda o: (o % FORC) * BLOCKS + o // FORC)
    state_ref[...] = dot(order, wide[...])[:, :DOF].astype(BF)


def place(back):
    return call(
        place_kernel, jax.ShapeDtypeStruct((ROWS, DOF), BF), [pltpu.VMEM((ROWS, WIDE), BF)], "place", 16, 2 * ROWS * ROWS * WIDE
    )(back)


def swaps(firsts):
    return [pair for i in firsts for pair in ((i, i + 1), (i + 1, i))]


def body(state, bits, couplings, shapes, amap):
    n_h, n_rad = lax.axis_size("h"), lax.axis_size("r")
    ahead = [(i, i + 1) for i in range(n_h - 1)]
    back = [(b, a) for a, b in ahead]

    send = pack(state.reshape(ROWS, DOF), bits.transpose(0, 2, 1))
    mine = lax.all_to_all(send, ("y", "r"), 0, 0, tiled=True)
    reach = HALO // AXB * n_rad
    low = lax.ppermute(mine[-reach:], "h", ahead)
    high = lax.ppermute(mine[:reach], "h", back)
    fore, adj, keep, masks = inner(mine, couplings)
    lower = outer(False, low, keep, masks, fore, adj)
    out = outer(True, high, keep, masks, fore, adj, lower)
    back_home = lax.all_to_all(out, ("y", "r"), 0, 0, tiled=True)

    for_far, for_near, own = project(back_home, shapes.reshape(BLOCKS, DOF), amap)
    n_ax = n_h * RING
    from_far = lax.ppermute(for_far, ("h", "y"), swaps(range(1, n_ax - 1, 2)))
    from_near = lax.ppermute(for_near, ("h", "y"), swaps(range(0, n_ax - 1, 2)))
    result = place(back_home)
    return result.reshape(state.shape), (own + from_far + from_near).T


def solution(mesh):
    n_ax, n_rad = mesh.shape["ax"], mesh.shape["rad"]
    fine = Mesh(mesh.devices.reshape(n_ax // RING, RING, n_rad), ("h", "y", "r"))
    ax = ("h", "y")
    in_specs = (P(ax, "r"), P(ax, "r"), P(), P(ax, "r"), P(ax, "r"))
    out_specs = (P(ax, "r"), P(None, ("h", "y", "r")))
    return jax.shard_map(body, mesh=fine, in_specs=in_specs, out_specs=out_specs, check_vma=False)
```

```python
import functools

import jax
import jax.numpy as jnp
from jax import lax
from jax.experimental import pallas as pl
from jax.experimental.pallas import tpu as pltpu
from jax.sharding import Mesh, PartitionSpec as P

ACT = 4096
STEPS = 2
DOF = 320
FORC = 16
RING = 4
AXB = 2
RADB = 16
BLOCKS = AXB * RADB
WIDE = 384
MAIN = 256
HALO = 2 * STEPS
BF = jnp.bfloat16
F32 = jnp.float32
ROWS = FORC * BLOCKS
NRAD = 4
LINE = NRAD * RADB
WINDOW = RING * AXB + 2 * HALO
DEPTH = 5 * MAIN + WIDE
PACKED = 80


def iota(shape, dim):
    return lax.broadcasted_iota(jnp.int32, shape, dim)


def one_hot(rows, cols, of_row):
    return jnp.where(iota((rows, cols), 1) == of_row(iota((rows, cols), 0)), 1.0, 0.0).astype(BF)


def dot(a, b):
    return jnp.dot(a, b, preferred_element_type=F32)


def dot_nt(a, b):
    return lax.dot_general(a, b, (((1,), (1,)), ((), ())), preferred_element_type=F32)


def call(kernel, out_shape, scratch_shapes, name, mib, flops, in_specs=None):
    return pl.pallas_call(
        kernel,
        out_shape=out_shape,
        **({} if in_specs is None else {"in_specs": in_specs}),
        scratch_shapes=scratch_shapes,
        compiler_params=pltpu.CompilerParams(vmem_limit_bytes=mib * 1024 * 1024),
        cost_estimate=pl.CostEstimate(flops=flops, bytes_accessed=2 * 1024 * 1024, transcendentals=0),
        name=name,
    )


def pack_kernel(state_ref, bits_ref, out_ref, rows, links, wide, bits, sems):
    copy = pltpu.make_async_copy(state_ref, rows, sems.at[0])
    link_copy = pltpu.make_async_copy(bits_ref, links, sems.at[1])
    link_copy.start()
    copy.start()
    order = one_hot(ROWS, ROWS, lambda o: (o % BLOCKS) * FORC + o // BLOCKS)
    bits[...] = jnp.zeros_like(bits)
    wide[:, MAIN:] = jnp.zeros((ROWS, 128), BF)
    link_copy.wait()
    for a in range(AXB):
        bits[a, 64:68, :RADB] = links[a].astype(F32)
    spread = [dot_nt(one_hot(ROWS, 128, lambda o: o % BLOCKS - a * RADB), bits[a].astype(BF)) for a in range(AXB)]
    copy.wait()
    wide[:, :DOF] = rows[...]
    out = dot(order, wide[...]).astype(BF)
    meta = (spread[0] + spread[1]).astype(BF)
    out_ref[:, :, :MAIN] = out[:, :MAIN].reshape(FORC, BLOCKS, MAIN)
    out_ref[:, :, MAIN:] = (out[:, MAIN:] + meta).reshape(FORC, BLOCKS, 128)


def pack(state, bits):
    return call(
        pack_kernel,
        jax.ShapeDtypeStruct((FORC, BLOCKS, WIDE), BF),
        [
            pltpu.VMEM((ROWS, DOF), BF),
            pltpu.VMEM((AXB, 4, RADB), jnp.int32),
            pltpu.VMEM((ROWS, WIDE), BF),
            pltpu.VMEM((AXB, 128, 128), F32),
            pltpu.SemaphoreType.DMA((2,)),
        ],
        "pack",
        16,
        2 * ROWS * ROWS * WIDE,
        [pl.BlockSpec(memory_space=pltpu.HBM)] * 2,
    )(state, bits)


def stack_weights(couplings_ref, fore_ref, adj_ref):
    twice = jnp.where(
        (iota((DOF, WIDE), 1) == iota((DOF, WIDE), 0)) | (iota((DOF, WIDE), 1) == iota((DOF, WIDE), 0) + 64)
        & (iota((DOF, WIDE), 1) >= DOF),
        1.0,
        0.0,
    ).astype(BF)
    same = one_hot(DOF, DOF, lambda o: o)

    def put(ref, at, value):
        ref[at * MAIN : (at + 1) * MAIN, :] = value[:MAIN].astype(BF)
        ref[5 * MAIN + at * 64 : 5 * MAIN + (at + 1) * 64, :] = value[MAIN:].astype(BF)

    for at in range(5):
        matrix = couplings_ref[at]
        tail = dot(matrix, twice[:, MAIN:]).astype(BF)
        fore_ref[at * MAIN : (at + 1) * MAIN, :MAIN] = matrix[:MAIN, :MAIN]
        fore_ref[at * MAIN : (at + 1) * MAIN, MAIN:] = tail[:MAIN]
        fore_ref[5 * MAIN + at * 64 : 5 * MAIN + (at + 1) * 64, :MAIN] = matrix[MAIN:, :MAIN]
        fore_ref[5 * MAIN + at * 64 : 5 * MAIN + (at + 1) * 64, MAIN:] = tail[MAIN:]
    for at, e in enumerate((0, 2, 1, 4, 3)):
        matrix = couplings_ref[e]
        put(adj_ref, at, dot_nt(same, jnp.concatenate([matrix, matrix[MAIN:]], axis=0)))
    for ref in (fore_ref, adj_ref):
        ref[DEPTH - 64 :, :] = jnp.zeros((64, WIDE), BF)


def put_rows(ref, row, source, slot, half):
    for r in range(NRAD):
        ref[row * LINE + r * RADB : row * LINE + (r + 1) * RADB, :] = source[slot + r, half * RADB : (half + 1) * RADB, :]


def spread_bits(field, masks, first, last):
    a, b = first * LINE, last * LINE
    pick = jnp.where(iota((128, 512), 0) == 64 + iota((128, 512), 1) // 128, 1.0, 0.0).astype(BF)
    tail = field[a:b, MAIN:]
    spread = dot(tail, pick)
    place = iota((b - a, 128), 0) % LINE
    masks[a:b, :256] = spread[:, :256].astype(BF)
    masks[a:b, 256:384] = jnp.where(place > 0, spread[:, 256:384], 0.0).astype(BF)
    masks[a:b, 384:] = jnp.where(place < LINE - 1, spread[:, 384:], 0.0).astype(BF)
    tail = tail.astype(F32)
    tail = jnp.where(iota((b - a, 128), 1) < 64, tail, pltpu.roll(tail, 64, 1))
    field[a:b, MAIN:] = tail.astype(BF)


def sides(value, masks, left, right, first, last):
    a, b = first * LINE, last * LINE
    down, up = pltpu.roll(value, 1, 0).astype(BF), pltpu.roll(value, b - a - 1, 0).astype(BF)
    for t in range(3):
        cols = slice(128 * t, 128 * t + 128)
        left[a:b, cols] = down[:, cols] * masks[a:b, 256:384]
        right[a:b, cols] = up[:, cols] * masks[a:b, 384:]


def stencil(field, masks, left, right, weights, first, last):
    a, b = first * LINE, last * LINE
    first_half = iota((b - a, 128), 1) < 64
    m0, m1 = masks[a:b, :128], masks[a:b, 128:256]
    prev, own, nxt = field[a - LINE : b - LINE, :], field[a:b, :], field[a + LINE : b + LINE, :]
    lhs = jnp.concatenate(
        [
            own[:, :MAIN],
            prev[:, :128] * m0,
            prev[:, 128:256] * m0,
            nxt[:, :128] * m1,
            nxt[:, 128:256] * m1,
            left[a:b, :MAIN],
            right[a:b, :MAIN],
            jnp.where(first_half, own[:, MAIN:], prev[:, MAIN:] * m0),
            jnp.where(first_half, nxt[:, MAIN:] * m1, left[a:b, MAIN:]),
            right[a:b, MAIN:],
        ],
        axis=1,
    )
    return dot(lhs, weights[...])


KEEP = []
for level in range(4):
    lo, hi = HALO + level, WINDOW - HALO - 1 - level
    edge = [lo, lo + 1, hi - 1, hi] if level < 3 else [lo, hi]
    KEEP += [(0, level, row) for row in edge]
    KEEP += [(side, level, row) for side in (1, 2) for row in (lo, hi)]
INNER = WINDOW - 2 * HALO


def inner_kernel(mine_ref, couplings_ref, fore_ref, adj_ref, keep_ref, mask_ref, s_a, s_b, left, right):
    stack_weights(couplings_ref, fore_ref, adj_ref)
    for i in range(INNER):
        put_rows(s_a, i, mine_ref, (i // AXB) * NRAD, i % AXB)
    spread_bits(s_a, mask_ref, 0, INNER)
    sides(s_a[...].astype(F32), mask_ref, left, right, 0, INNER)

    def keep(level, field):
        for at, (kind, of, row) in enumerate(KEEP):
            if of == level:
                a = (row - HALO) * LINE
                keep_ref[at * LINE : (at + 1) * LINE, :] = (field, left, right)[kind][a : a + LINE, :]

    keep(0, s_a)
    now, later = s_a, s_b
    for level in range(1, 4):
        first, last = level, INNER - level
        value = stencil(now, mask_ref, left, right, fore_ref if level <= STEPS else adj_ref, first, last)
        later[first * LINE : last * LINE, :] = value.astype(BF)
        sides(value, mask_ref, left, right, first, last)
        keep(level, later)
        now, later = later, now


def inner(mine, couplings):
    field = pltpu.VMEM((INNER * LINE, WIDE), BF)
    weights = jax.ShapeDtypeStruct((DEPTH, WIDE), BF)
    return call(
        inner_kernel,
        (weights, weights, jax.ShapeDtypeStruct((len(KEEP) * LINE, WIDE), BF), jax.ShapeDtypeStruct((INNER * LINE, 512), BF)),
        [field, field, field, field],
        "inner",
        24,
        2 * 12 * LINE * DEPTH * WIDE,
    )(mine, couplings)


def outer_kernel(upper, *refs):
    halo_ref, keep_ref, mask_ref, fore_ref, adj_ref = refs[:5]
    out_ref, s_a, s_b, left, right, masks = refs[-6:]
    edge = WINDOW - HALO if upper else 0
    for i in range(HALO):
        put_rows(s_a, edge + i, halo_ref, (i // AXB) * NRAD, i % AXB)
    half = WINDOW // 2 if upper else HALO
    at = (half - HALO) * LINE
    masks[half * LINE : (half + HALO) * LINE, :] = mask_ref[at : at + HALO * LINE, :]
    spread_bits(s_a, masks, edge, edge + HALO)
    sides(s_a[edge * LINE : (edge + HALO) * LINE, :].astype(F32), masks, left, right, edge, edge + HALO)

    now, later = s_a, s_b
    for level in range(4):
        for at, (kind, of, row) in enumerate(KEEP):
            if of == level:
                (now, left, right)[kind][row * LINE : (row + 1) * LINE, :] = keep_ref[at * LINE : (at + 1) * LINE, :]
        first = WINDOW - HALO - 1 - level if upper else level + 1
        last = first + HALO
        value = stencil(now, masks, left, right, fore_ref if level < STEPS else adj_ref, first, last)
        later[first * LINE : last * LINE, :] = value.astype(BF)
        if level < 3:
            sides(value, masks, left, right, first, last)
        now, later = later, now

    early = iota((RADB, 128), 1) < 64
    slots = FORC // 2
    if upper:
        out_ref[:slots] = refs[5][...]
    for slot in range(slots):
        y, r = slot // NRAD, slot % NRAD
        rows = [(half + y * AXB + a) * LINE + r * RADB for a in range(AXB)]
        to = slot + (slots if upper else 0)
        for a, row in enumerate(rows):
            out_ref[to, a * RADB : (a + 1) * RADB, :] = now[row : row + RADB, :128]
            out_ref[to, BLOCKS + a * RADB : BLOCKS + (a + 1) * RADB, :] = now[row : row + RADB, 128:256]
        out_ref[to, 2 * BLOCKS :, :] = jnp.where(early, now[rows[0] : rows[0] + RADB, MAIN:], now[rows[1] : rows[1] + RADB, MAIN:])


def outer(upper, *args):
    field = pltpu.VMEM((WINDOW * LINE, WIDE), BF)
    return call(
        functools.partial(outer_kernel, upper),
        jax.ShapeDtypeStruct((FORC if upper else FORC // 2, PACKED, 128), BF),
        [field, field, field, field, pltpu.VMEM((WINDOW * LINE, 512), BF)],
        "upper" if upper else "lower",
        24,
        2 * 16 * LINE * DEPTH * WIDE,
    )(*args)


def project_kernel(back_ref, shapes_ref, map_ref, far_ref, near_ref, own_ref):
    y = lax.axis_index("y")
    group = (lax.axis_index("h") * RING + y) * NRAD + lax.axis_index("r")
    actuator = map_ref[...]
    column = (((((actuator >> 2) - group) >> 2) + 1) * 4 + (actuator & 3)).astype(F32)
    same = iota((RADB, RADB), 0) == iota((RADB, RADB), 1)
    column = jnp.concatenate(
        [jnp.sum(jnp.where(same, column[a : a + 1, :], 0.0), axis=1, keepdims=True) for a in range(AXB)], axis=0
    )
    shapes = shapes_ref[...].astype(F32)
    tails = jnp.concatenate([shapes[:RADB, MAIN:], shapes[RADB:, MAIN:]], axis=1)
    back = back_ref[...].astype(F32)
    body_sum = back[:, :BLOCKS] * shapes[None, :, :128] + back[:, BLOCKS : 2 * BLOCKS] * shapes[None, :, 128:256]
    tail = back[:, 2 * BLOCKS :] * tails[None]
    early = iota((FORC, RADB, 128), 2) < 64
    tail = jnp.concatenate([jnp.where(early, tail, 0.0), jnp.where(early, 0.0, tail)], axis=1)
    proj = jnp.sum(body_sum + tail, axis=2, keepdims=True)
    lane = iota((BLOCKS, 128), 1)
    by_block = jnp.zeros((BLOCKS, 128), F32)
    for f in range(FORC):
        by_block = jnp.where(lane == f, proj[f], by_block)
    parts = [
        [jnp.sum(jnp.where(column == 4 * at + slot, by_block, 0.0), axis=0, keepdims=True)[:, :FORC] for slot in range(4)]
        for at in range(3)
    ]
    odd = jnp.broadcast_to(y % 2, (1, FORC)) == 1
    for slot in range(4):
        to_prev, own, to_next = [part[slot] for part in parts]
        far_ref[slot : slot + 1, :] = jnp.where(odd, to_next, to_prev)
        near_ref[slot : slot + 1, :] = jnp.where(odd, to_prev, to_next)
        own_ref[slot : slot + 1, :] = own


def project(back, shapes, amap):
    part = jax.ShapeDtypeStruct((4, FORC), F32)
    return call(project_kernel, (part, part, part), [], "project", 16, 2 * ROWS * DOF)(back, shapes, amap)


def place_kernel(back_ref, state_ref, wide):
    for f in range(FORC):
        row = f * BLOCKS
        wide[row : row + BLOCKS, :128] = back_ref[f, :BLOCKS, :]
        wide[row : row + BLOCKS, 128:256] = back_ref[f, BLOCKS : 2 * BLOCKS, :]
        tail = back_ref[f, 2 * BLOCKS :, :]
        wide[row : row + RADB, MAIN:] = tail
        wide[row + RADB : row + BLOCKS, MAIN:] = pltpu.roll(tail.astype(F32), 64, 1).astype(BF)
    order = one_hot(ROWS, ROWS, lambda o: (o % FORC) * BLOCKS + o // FORC)
    state_ref[...] = dot(order, wide[...])[:, :DOF].astype(BF)


def place(back):
    return call(
        place_kernel, jax.ShapeDtypeStruct((ROWS, DOF), BF), [pltpu.VMEM((ROWS, WIDE), BF)], "place", 16, 2 * ROWS * ROWS * WIDE
    )(back)


def swaps(firsts):
    return [pair for i in firsts for pair in ((i, i + 1), (i + 1, i))]


def body(state, bits, couplings, shapes, amap):
    n_h, n_rad = lax.axis_size("h"), lax.axis_size("r")
    ahead = [(i, i + 1) for i in range(n_h - 1)]
    back = [(b, a) for a, b in ahead]

    send = pack(state.reshape(ROWS, DOF), bits.transpose(0, 2, 1))
    mine = lax.all_to_all(send, ("y", "r"), 0, 0, tiled=True)
    reach = HALO // AXB * n_rad
    low = lax.ppermute(mine[-reach:], "h", ahead)
    high = lax.ppermute(mine[:reach], "h", back)
    fore, adj, keep, masks = inner(mine, couplings)
    lower = outer(False, low, keep, masks, fore, adj)
    out = outer(True, high, keep, masks, fore, adj, lower)
    back_home = lax.all_to_all(out, ("y", "r"), 0, 0, tiled=True)

    for_far, for_near, own = project(back_home, shapes.reshape(BLOCKS, DOF), amap)
    n_ax = n_h * RING
    from_far = lax.ppermute(for_far, ("h", "y"), swaps(range(1, n_ax - 1, 2)))
    from_near = lax.ppermute(for_near, ("h", "y"), swaps(range(0, n_ax - 1, 2)))
    result = place(back_home)
    return result.reshape(state.shape), (own + from_far + from_near).T


def solution(mesh):
    n_ax, n_rad = mesh.shape["ax"], mesh.shape["rad"]
    fine = Mesh(mesh.devices.reshape(n_ax // RING, RING, n_rad), ("h", "y", "r"))
    ax = ("h", "y")
    in_specs = (P(ax, "r"), P(ax, "r"), P(), P(ax, "r"), P(ax, "r"))
    out_specs = (P(ax, "r"), P(None, ("h", "y", "r")))
    return jax.shard_map(body, mesh=fine, in_specs=in_specs, out_specs=out_specs, check_vma=False)
```
